32 devices in a mesh: groups: 1, seq: 32 (over z, y, x, core), fsdp: 1.
Axes of the slice: x: 2, y: 2, z: 4, core: 2. Of those that a mesh axis runs over, the one named last changes fastest.
Arguments:
- fine: bfloat16 [4096, 1024], P(('groups', 'seq'), 'fsdp'), may hold values from -3 to 3
- queries: bfloat16 [4096, 1024], P(('groups', 'seq'), 'fsdp'), may hold values from -180 to 180
- keys: bfloat16 [512, 1024], P(('groups', 'seq'), 'fsdp'), may hold values from -6 to 6
- values: bfloat16 [512, 1024], P(('groups', 'seq'), 'fsdp'), may hold values from -24 to 24
- pattern: int32 [32, 2], P(('groups', 'seq')), may hold values from 0 to 3, as said below
- counts: int32 [32], P(('groups', 'seq')), may hold values from 1 to 2, as said below
- norm_gain: float32 [1024], replicated, may hold values from 0.1 to 1.9
- w_in: bfloat16 [1024, 2048], P('fsdp'), may hold values from -0.1875 to 0.1875
- w_out: bfloat16 [2048, 1024], P('fsdp'), may hold values from -0.125 to 0.125
Outputs:
- mixed: bfloat16 [4096, 1024], P(('groups', 'seq', 'fsdp'))
The draws below stay inside these ranges and needn't reach their ends.
Inputs may be any that keep to these rules, and one draw needn't show every extreme that they name: `pattern`: the 2 entries of a row are different key blocks; the first is the block that holds coarse row (b * 128) // 8 for query block b. The query blocks of one index of seq have counts that differ by at most one; on some index of seq every query block has 2.
All inputs are finite; a program needn't handle non-finite values.
Results may differ from the reference program's by a relative error of at most 0.0065.
Values may be sent and summed in bfloat16 or wider, within the bound.
A program may use at most 64 MiB of HBM per device.

```python
import jax
import jax.numpy as jnp
from jax import lax

D = 1024
HEADS = 16
HEAD = 64
FF = 2048
SHORTEN = 8
QBLK = 128
KBLK = 128
F_DEV = 128
TOKENS = 4096
CTOK = 512
QBLOCKS = 32
KBLOCKS = 4
KSLOTS = 2


def shared_fields(key):
    key_rows = jnp.clip(jax.random.normal(jax.random.fold_in(key, 11), (CTOK, D), jnp.float32), -6.0, 6.0)
    return key_rows


def draw_keys(key, part):
    return shared_fields(key).astype(jnp.bfloat16)


def draw_queries(key, part):
    result = jnp.clip(jax.random.normal(jax.random.fold_in(key, 12), (TOKENS, D), jnp.float32), -6.0, 6.0)
    return result.astype(jnp.bfloat16)


def draw_pattern(key, part):
    block_ids = jnp.arange(QBLOCKS, dtype=jnp.int32)
    own_block = block_ids * QBLK // SHORTEN // KBLK
    random_scores = jax.random.randint(jax.random.fold_in(key, 31), (QBLOCKS, KBLOCKS - 1), 0, 1 << 20) * KBLOCKS + jnp.arange(KBLOCKS - 1, dtype=jnp.int32)[None, :]
    top_values, picked = lax.top_k(random_scores, KSLOTS - 1)
    others = (own_block[:, None] + 1 + picked.astype(jnp.int32)) % KBLOCKS
    return jnp.concatenate([own_block[:, None], others], axis=1).astype(jnp.int32)


def draw_counts(key, part):
    per_shard = F_DEV // QBLK
    shards = QBLOCKS // per_shard
    draw_rough = jax.random.randint(jax.random.fold_in(key, 21), (shards,), 0, KSLOTS)
    levels = 1 + draw_rough * draw_rough // KSLOTS
    busiest = jax.random.randint(jax.random.fold_in(key, 22), (), 0, shards)
    is_busy = jnp.arange(shards, dtype=jnp.int32) == busiest
    levels = jnp.where(is_busy, KSLOTS, levels)
    owners = jnp.arange(QBLOCKS, dtype=jnp.int32) // per_shard
    jitter = jax.random.randint(jax.random.fold_in(key, 23), (QBLOCKS,), 0, 2)
    result = levels[owners] - jitter * (1 - is_busy[owners].astype(jnp.int32))
    return jnp.clip(result, 1, KSLOTS).astype(jnp.int32)


def block_levels(own_key, dims, cuts, smallest, high):
    factor_of = 1.0
    for position, shards_of in cuts:
        heights = jax.random.uniform(jax.random.fold_in(jax.random.fold_in(own_key, 6), position), (shards_of,), jnp.float32, smallest / len(cuts), high / len(cuts))
        factor_of = factor_of * jnp.repeat(jnp.exp(heights), dims[position] // shards_of).reshape((-1,) + (1,) * (len(dims) - 1 - position))
    return factor_of


def centred(own_key, extent, deviation, bound, split=(), kind=jnp.bfloat16):
    drawn = jax.random.normal(own_key, extent, jnp.float32) * deviation
    if len(split) > 0:
        drawn = block_levels(own_key, extent, split, -0.22, 0.18) * drawn
    return jnp.clip(drawn, min=-bound, max=bound).astype(kind)


def setup_inputs(seed: int = 0, part: int = 0) -> dict:
    key_list = jax.random.split(jax.random.key(seed), 10)
    part_keys = jax.random.split(jax.random.fold_in(key_list[9], part), 10)
    fine = centred(part_keys[0], (TOKENS, D), 0.5, 3.0, ((0, 32),))
    queries = draw_queries(jax.random.fold_in(jax.random.fold_in(key_list[9], part), 71), part)
    keys = draw_keys(jax.random.fold_in(jax.random.fold_in(key_list[9], part), 71), part)
    values = centred(part_keys[3], (CTOK, D), 4.0, 24.0, ((0, 32),))
    pattern = draw_pattern(jax.random.fold_in(jax.random.fold_in(key_list[9], part), 71), part)
    counts = draw_counts(jax.random.fold_in(jax.random.fold_in(key_list[9], part), 71), part)
    norm_gain = jnp.clip(1.0 + 0.18 * jax.random.normal(key_list[6], (D,), jnp.float32), 0.1, 1.9)
    w_in = centred(key_list[7], (D, FF), D ** -0.5, 0.1875)
    w_out = centred(key_list[8], (FF, D), FF ** -0.5, 0.125)
    return dict(fine=fine, queries=queries, keys=keys, values=values, pattern=pattern, counts=counts, norm_gain=norm_gain, w_in=w_in, w_out=w_out)


def attend_block(arguments, key_blocks, value_blocks):
    query_block, listed, used = arguments
    scale_factor = 1.0 / HEAD ** 0.5
    key_rows = key_blocks[listed].reshape(KSLOTS * KBLK, HEADS, HEAD).astype(jnp.float32)
    value_rows = value_blocks[listed].reshape(KSLOTS * KBLK, HEADS, HEAD).astype(jnp.float32)
    allowed = jnp.repeat(jnp.arange(KSLOTS, dtype=jnp.int32) < used, KBLK)
    scores = jnp.einsum('qhd,khd->hqk', query_block.astype(jnp.float32), key_rows) * scale_factor
    largest = lax.optimization_barrier(jnp.max(jnp.where(allowed[None, None, :], scores, -1e+30), axis=2, keepdims=True))
    probs = jnp.where(allowed[None, None, :], jnp.exp(jnp.where(allowed[None, None, :], scores - largest, -1e+30)), 0.0)
    totals = lax.optimization_barrier(jnp.sum(probs, axis=2, keepdims=True))
    rounded = lax.optimization_barrier(probs.astype(jnp.bfloat16)).astype(jnp.float32)
    summed = jnp.einsum('hqk,khd->qhd', rounded, value_rows)
    return (summed / jnp.transpose(totals, (1, 0, 2))).astype(jnp.bfloat16)

def reference(fine, queries, keys, values, pattern, counts, norm_gain, w_in, w_out):
    key_blocks = keys.reshape(KBLOCKS, KBLK, HEADS, HEAD)
    value_blocks = values.reshape(KBLOCKS, KBLK, HEADS, HEAD)
    query_blocks = queries.reshape(QBLOCKS, QBLK, HEADS, HEAD)
    attn = lax.map(lambda arguments: attend_block(arguments, key_blocks, value_blocks), (query_blocks, pattern, counts))
    attn = attn.reshape(TOKENS, D)
    middle = fine.astype(jnp.float32) + attn.astype(jnp.float32)
    mean_square = lax.optimization_barrier(jnp.mean(middle * middle, axis=1, keepdims=True))
    normed = (middle * lax.rsqrt(mean_square + 1e-06) * norm_gain).astype(jnp.bfloat16)
    hidden = jax.nn.gelu(jnp.dot(normed, w_in, preferred_element_type=jnp.float32), approximate=True).astype(jnp.bfloat16)
    return (middle + jnp.dot(hidden, w_out, preferred_element_type=jnp.float32)).astype(jnp.bfloat16)
```

```python
import functools
import math

import jax
import jax.numpy as jnp
from jax import lax
from jax.experimental import pallas as pl
from jax.experimental.pallas import tpu as pltpu
from jax.sharding import PartitionSpec as P

HEAD = 64
QBLK = 128
KBLK = 128
MESH = pl.DeviceIdType.MESH
PLANE = 8
LEVELS = 4


def choose(ref, others, picks, columns):
    block = None
    for start, pick in zip(others, picks):
        part = ref[pl.ds(start, KBLK), columns] * pick
        block = part if block is None else block + part
    return block


def attend_pair(q_ref, k_ref, v_ref, fine_ref, mid_ref, own, others, picks, bias, pair):
    columns = pl.ds(pair * 2 * HEAD, 2 * HEAD)
    q = q_ref[:, columns] * jnp.bfloat16(1.0 / math.sqrt(HEAD))
    lane = lax.broadcasted_iota(jnp.int32, q.shape, 1)
    zero = jnp.zeros_like(q)
    both = jnp.concatenate([jnp.where(lane < HEAD, q, zero), jnp.where(lane < HEAD, zero, q)], axis=0)
    k = jnp.concatenate([k_ref[pl.ds(own, KBLK), columns], choose(k_ref, others, picks, columns)], axis=0)
    s = lax.dot_general(both, k, (((1,), (1,)), ((), ())), preferred_element_type=jnp.float32) + bias
    top = jnp.max(s, axis=1, keepdims=True)
    weights = jnp.exp(s - top).astype(jnp.bfloat16)
    v = jnp.concatenate([v_ref[pl.ds(own, KBLK), columns], choose(v_ref, others, picks, columns)], axis=0)
    v = jnp.concatenate([v, jnp.ones_like(v)], axis=1)
    summed = jnp.dot(weights, v, preferred_element_type=jnp.float32)
    out = summed[:, : 2 * HEAD] / summed[:, 2 * HEAD :]
    rows = q.shape[0]
    out = jnp.where(lane < HEAD, out[:rows], out[rows:]).astype(jnp.bfloat16)
    mid_ref[:, columns] = fine_ref[:, columns].astype(jnp.float32) + out.astype(jnp.float32)


def feed_forward(mid_ref, gain_ref, win, wout, hid_ref, out_ref, wait_in, wait_out):
    mid = mid_ref[...]
    mean_square = jnp.mean(mid * mid, axis=1, keepdims=True)
    normed = (mid * lax.rsqrt(mean_square + 1e-06) * gain_ref[...]).astype(jnp.bfloat16)
    wait_in()
    step = 256
    for c in range(hid_ref.shape[1] // step):
        cols = pl.ds(c * step, step)
        before = jnp.dot(normed, win[:, cols], preferred_element_type=jnp.float32)
        hid_ref[:, cols] = jax.nn.gelu(before, approximate=True).astype(jnp.bfloat16)
    wait_out()
    for c in range(out_ref.shape[1] // step):
        cols = pl.ds(c * step, step)
        y = jnp.dot(hid_ref[...], wout[:, cols], preferred_element_type=jnp.float32)
        out_ref[:, cols] = (mid_ref[:, cols] + y).astype(jnp.bfloat16)


def kernel(
    pattern_hbm, counts_hbm, q_hbm, k_ref, v_ref, fine_hbm, gain_hbm, win_hbm, wout_hbm,
    out_ref,
    pattern_ref, counts_ref, q_ref, fine_ref, gain_ref, kg, vg, win, wout, mid, hid, load_sem, send_sem, recv_sem,
):
    me = lax.axis_index("seq")
    shard = k_ref.shape[0]
    z, y, x, c = me // PLANE, (me // 4) % 2, (me // 2) % 2, me % 2

    def at(zz, yy, xx, cc):
        return zz * PLANE + yy * 4 + xx * 2 + cc

    zs = [(z + d) % LEVELS for d in (0, 1, 3, 2)]
    x_nbr, y_nbr, core = at(z, y, 1 - x, c), at(z, 1 - y, x, c), at(z, y, x, 1 - c)
    z_nbrs = [at(zz, y, x, c) for zz in zs[1:]]

    barrier = pltpu.get_barrier_semaphore()
    greeted = [x_nbr, y_nbr, core] + z_nbrs
    for other in greeted:
        pl.semaphore_signal(barrier, inc=1, device_id={"seq": other}, device_id_type=MESH)
    own_rows = pl.ds(pl.multiple_of(me * shard, shard), shard)
    moves = [
        (k_ref, kg.at[own_rows, :]), (v_ref, vg.at[own_rows, :]), (q_hbm, q_ref), (pattern_hbm, pattern_ref),
        (counts_hbm, counts_ref), (fine_hbm, fine_ref), (gain_hbm, gain_ref), (win_hbm, win), (wout_hbm, wout),
    ]
    loads = [pltpu.make_async_copy(a, b, load_sem.at[i]) for i, (a, b) in enumerate(moves)]
    for load in loads:
        load.start()
    pl.semaphore_wait(barrier, len(greeted))

    gathered = (kg, vg)
    sent = []

    def rows_of(origin):
        return pl.ds(pl.multiple_of(origin * shard, shard), shard)

    def copy_of(kind, origin, target, own=False):
        place = gathered[kind].at[rows_of(origin), :]
        source = (k_ref, v_ref)[kind] if own else place
        return pltpu.make_async_remote_copy(
            src_ref=source, dst_ref=place,
            send_sem=send_sem.at[len(sent)], recv_sem=recv_sem.at[kind, origin],
            device_id={"seq": target}, device_id_type=MESH,
        )

    def send(kind, origin, target, own=False):
        copy = copy_of(kind, origin, target, own)
        copy.start()
        sent.append(copy)

    def arrive(kind, origin):
        pltpu.make_async_remote_copy(
            src_ref=gathered[kind].at[rows_of(origin), :], dst_ref=gathered[kind].at[rows_of(origin), :],
            send_sem=send_sem.at[0], recv_sem=recv_sem.at[kind, origin],
            device_id={"seq": core}, device_id_type=MESH,
        ).wait_recv()

    def column(level):
        origin = at(zs[level], y, x, c)
        own = level == 0
        for kind in (0, 1):
            if not own:
                arrive(kind, origin)
            for target in (x_nbr, y_nbr, core):
                send(kind, origin, target, own)

    def beside(level):
        by_y, by_x = at(zs[level], 1 - y, x, c), at(zs[level], y, 1 - x, c)
        arrive(0, by_y)
        send(0, by_y, x_nbr)
        send(0, by_y, core)
        arrive(0, by_x)
        send(0, by_x, core)
        arrive(1, by_x)
        send(1, by_x, y_nbr)
        send(1, by_x, core)
        arrive(1, by_y)
        send(1, by_y, core)

    def across(level):
        origin = at(zs[level], 1 - y, 1 - x, c)
        for kind in (0, 1):
            arrive(kind, origin)
            send(kind, origin, core)

    for kind in (0, 1):
        for target in z_nbrs:
            send(kind, me, target, True)
    for turn in range(LEVELS + 2):
        if turn < LEVELS:
            column(turn)
        if 0 <= turn - 1 < LEVELS:
            beside(turn - 1)
        if 0 <= turn - 2 < LEVELS:
            across(turn - 2)
    for zz in zs:
        for yy in (y, 1 - y):
            for xx in (x, 1 - x):
                for kind in (0, 1):
                    arrive(kind, at(zz, yy, xx, 1 - c))

    for load in loads[:6]:
        load.wait()
    own = pl.multiple_of(z * KBLK, KBLK)
    others = [pl.multiple_of(zz * KBLK, KBLK) for zz in zs[1:]]
    second = jnp.broadcast_to(pattern_ref[:, 1:2], (1, 2 * HEAD))
    picks = [jnp.where(second == zz, 1.0, 0.0).astype(jnp.bfloat16) for zz in zs[1:]]
    used = jnp.broadcast_to(counts_ref[...], (1, KBLK))
    bias = jnp.concatenate([jnp.zeros((1, KBLK), jnp.float32), jnp.where(used > 1, 0.0, -1e30)], axis=1)
    for pair in range(q_ref.shape[1] // (2 * HEAD)):
        attend_pair(q_ref, kg, vg, fine_ref, mid, own, others, picks, bias, pair)
    loads[6].wait()
    feed_forward(mid, gain_ref, win, wout, hid, out_ref, loads[7].wait, loads[8].wait)
    for copy in sent:
        copy.wait_send()


def fast_shards(fine, queries, keys, values, pattern, counts, norm_gain, w_in, w_out):
    rows, width = fine.shape
    hidden = w_in.shape[1]
    gathered = (keys.shape[0] * lax.axis_size("seq"), width)
    vmem = pl.BlockSpec(memory_space=pltpu.VMEM)
    hbm = pl.BlockSpec(memory_space=pl.ANY)
    sends = 6 + LEVELS * (6 + 6 + 2)
    return pl.pallas_call(
        kernel,
        out_shape=jax.ShapeDtypeStruct((rows, width), jnp.bfloat16),
        in_specs=[hbm] * 9,
        out_specs=vmem,
        scratch_shapes=[
            pltpu.VMEM(pattern.shape, jnp.int32),
            pltpu.VMEM((1, 1), jnp.int32),
            pltpu.VMEM(queries.shape, jnp.bfloat16),
            pltpu.VMEM(fine.shape, jnp.bfloat16),
            pltpu.VMEM((1, width), jnp.float32),
            pltpu.VMEM(gathered, jnp.bfloat16),
            pltpu.VMEM(gathered, jnp.bfloat16),
            pltpu.VMEM(w_in.shape, jnp.bfloat16),
            pltpu.VMEM(w_out.shape, jnp.bfloat16),
            pltpu.VMEM((rows, width), jnp.float32),
            pltpu.VMEM((rows, hidden), jnp.bfloat16),
            pltpu.SemaphoreType.DMA((9,)),
            pltpu.SemaphoreType.DMA((sends,)),
            pltpu.SemaphoreType.DMA((2, gathered[0] // keys.shape[0])),
        ],
        compiler_params=pltpu.CompilerParams(
            collective_id=0, has_side_effects=True, vmem_limit_bytes=58 * 2**20
        ),
        cost_estimate=pl.CostEstimate(
            flops=4 * rows * width * hidden, bytes_accessed=4 * width * hidden, transcendentals=rows * hidden
        ),
    )(pattern, counts.reshape(1, 1), queries, keys, values, fine, norm_gain.reshape(1, -1), w_in, w_out)


def shards(fine, queries, keys, values, pattern, counts, norm_gain, w_in, w_out):
    local_rows, half_width = queries.shape
    head_count = half_width // HEAD
    scale_factor = 1.0 / math.sqrt(HEAD)
    query_heads = queries.reshape(local_rows, head_count, HEAD)
    slot_count = pattern.shape[1]
    block_total = keys.shape[0] * lax.axis_size("seq") // KBLK
    slot_live = jnp.arange(slot_count, dtype=jnp.int32)[None, :] < counts[:, None]
    block_ids = jnp.arange(block_total, dtype=jnp.int32)
    chosen = jnp.any(
        (pattern[:, :, None] == block_ids[None, None, :]) & slot_live[:, :, None], axis=1
    )

    def absorb(running, key_rows, value_rows, first_row):
        width = key_rows.shape[0]
        row_block = (first_row + jnp.arange(width, dtype=jnp.int32)) // KBLK
        allowed = jnp.any(
            chosen[:, None, :] & (row_block[:, None] == block_ids[None, :])[None, :, :], axis=2
        )
        allowed = jnp.repeat(allowed, QBLK, axis=0)[None, :, :]
        maxima, totals, weighted = running
        scores = (
            jnp.einsum(
                "qhd,khd->hqk",
                query_heads,
                key_rows.reshape(width, head_count, HEAD),
                preferred_element_type=jnp.float32,
            )
            * scale_factor
        )
        piece_max = jnp.max(jnp.where(allowed, scores, -1e30), axis=2)
        new_max = jnp.maximum(maxima, piece_max)
        probs = jnp.where(
            allowed, jnp.exp(jnp.where(allowed, scores - new_max[:, :, None], -1e30)), 0.0
        )
        factor = jnp.exp(maxima - new_max)
        totals = totals * factor + jnp.sum(probs, axis=2)
        update = jnp.einsum(
            "hqk,khd->qhd",
            probs.astype(jnp.bfloat16),
            value_rows.reshape(width, head_count, HEAD),
            preferred_element_type=jnp.float32,
        )
        weighted = weighted * jnp.transpose(factor)[:, :, None] + update
        return (new_max, totals, weighted)

    initial = (
        jnp.full((head_count, local_rows), -1e30, jnp.float32),
        jnp.zeros((head_count, local_rows), jnp.float32),
        jnp.zeros((local_rows, head_count, HEAD), jnp.float32),
    )
    key_piece = lax.all_gather(keys, "seq", axis=0, tiled=True)
    value_piece = lax.all_gather(values, "seq", axis=0, tiled=True)
    width = key_piece.shape[0]
    span = 512

    def inner(turn, state):
        offset = turn * span
        return absorb(
            state,
            lax.dynamic_slice_in_dim(key_piece, offset, span, 0),
            lax.dynamic_slice_in_dim(value_piece, offset, span, 0),
            offset,
        )

    maxima, totals, weighted = lax.fori_loop(0, width // span, inner, initial)
    attn = (
        (weighted / jnp.transpose(totals)[:, :, None])
        .astype(jnp.bfloat16)
        .reshape(local_rows, half_width)
    )
    moved_fine, moved_attn = (
        lax.all_to_all(fine, "fsdp", split_axis=0, concat_axis=1, tiled=True),
        lax.all_to_all(attn, "fsdp", split_axis=0, concat_axis=1, tiled=True),
    )
    middle = moved_fine.astype(jnp.float32) + moved_attn.astype(jnp.float32)
    mean_square = jnp.mean(middle * middle, axis=1, keepdims=True)
    normed = (middle * lax.rsqrt(mean_square + 1e-06) * norm_gain).astype(jnp.bfloat16)
    before = jnp.dot(
        normed, lax.all_gather(w_in, "fsdp", axis=0, tiled=True), preferred_element_type=jnp.float32
    )
    hidden = jax.nn.gelu(before, approximate=True).astype(jnp.bfloat16)
    output_sum = jnp.dot(
        hidden,
        lax.all_gather(w_out, "fsdp", axis=0, tiled=True),
        preferred_element_type=jnp.float32,
    )
    return (middle + output_sum).astype(jnp.bfloat16)

def is_small(mesh):
    return mesh.shape["groups"] == 1 and mesh.shape["fsdp"] == 1 and mesh.shape["seq"] == PLANE * LEVELS


def solution(mesh):
    return jax.shard_map(
        fast_shards if is_small(mesh) else shards,
        mesh=mesh,
        in_specs=(
            P(("groups", "seq"), "fsdp"),
            P(("groups", "seq"), "fsdp"),
            P(("groups", "seq"), "fsdp"),
            P(("groups", "seq"), "fsdp"),
            P(("groups", "seq"), None),
            P(("groups", "seq")),
            P(),
            P("fsdp", None),
            P("fsdp", None),
        ),
        out_specs=P(("groups", "seq", "fsdp"), None),
        check_vma=False,
    )
```

```python
import functools
import math

import jax
import jax.numpy as jnp
from jax import lax
from jax.experimental import pallas as pl
from jax.experimental.pallas import tpu as pltpu
from jax.sharding import PartitionSpec as P

HEAD = 64
QBLK = 128
KBLK = 128
MESH = pl.DeviceIdType.MESH
PLANE = 8
LEVELS = 4


def choose(ref, others, picks, columns):
    block = None
    for start, pick in zip(others, picks):
        part = ref[pl.ds(start, KBLK), columns] * pick
        block = part if block is None else block + part
    return block


def weigh_pair(q_ref, k_ref, weight_ref, own, others, picks, bias, pair):
    columns = pl.ds(pair * 2 * HEAD, 2 * HEAD)
    q = q_ref[:, columns] * jnp.bfloat16(1.0 / math.sqrt(HEAD))
    lane = lax.broadcasted_iota(jnp.int32, q.shape, 1)
    zero = jnp.zeros_like(q)
    both = jnp.concatenate([jnp.where(lane < HEAD, q, zero), jnp.where(lane < HEAD, zero, q)], axis=0)
    k = jnp.concatenate([k_ref[pl.ds(own, KBLK), columns], choose(k_ref, others, picks, columns)], axis=0)
    s = lax.dot_general(both, k, (((1,), (1,)), ((), ())), preferred_element_type=jnp.float32) + bias
    top = jnp.max(s, axis=1, keepdims=True)
    weight_ref[pair] = jnp.exp(s - top).astype(jnp.bfloat16)


def attend_pair(weight_ref, v_ref, fine_ref, mid_ref, own, others, picks, pair):
    columns = pl.ds(pair * 2 * HEAD, 2 * HEAD)
    weights = weight_ref[pair]
    v = jnp.concatenate([v_ref[pl.ds(own, KBLK), columns], choose(v_ref, others, picks, columns)], axis=0)
    v = jnp.concatenate([v, jnp.ones_like(v)], axis=1)
    summed = jnp.dot(weights, v, preferred_element_type=jnp.float32)
    out = summed[:, : 2 * HEAD] / summed[:, 2 * HEAD :]
    rows = fine_ref.shape[0]
    lane = lax.broadcasted_iota(jnp.int32, (rows, 2 * HEAD), 1)
    out = jnp.where(lane < HEAD, out[:rows], out[rows:]).astype(jnp.bfloat16)
    mid_ref[:, columns] = fine_ref[:, columns].astype(jnp.float32) + out.astype(jnp.float32)


def feed_forward(mid_ref, gain_ref, win, wout, hid_ref, out_ref, wait_in, wait_out):
    mid = mid_ref[...]
    mean_square = jnp.mean(mid * mid, axis=1, keepdims=True)
    normed = (mid * lax.rsqrt(mean_square + 1e-06) * gain_ref[...]).astype(jnp.bfloat16)
    wait_in()
    step = 256
    for c in range(hid_ref.shape[1] // step):
        cols = pl.ds(c * step, step)
        before = jnp.dot(normed, win[:, cols], preferred_element_type=jnp.float32)
        hid_ref[:, cols] = jax.nn.gelu(before, approximate=True).astype(jnp.bfloat16)
    wait_out()
    for c in range(out_ref.shape[1] // step):
        cols = pl.ds(c * step, step)
        y = jnp.dot(hid_ref[...], wout[:, cols], preferred_element_type=jnp.float32)
        out_ref[:, cols] = (mid_ref[:, cols] + y).astype(jnp.bfloat16)


def kernel(
    pattern_hbm, counts_hbm, q_hbm, k_ref, v_ref, fine_hbm, gain_hbm, win_hbm, wout_hbm,
    out_ref,
    pattern_ref, counts_ref, q_ref, fine_ref, gain_ref, kg, vg, win, wout, mid, hid, weights, load_sem, send_sem, recv_sem,
):
    me = lax.axis_index("seq")
    shard = k_ref.shape[0]
    z, y, x, c = me // PLANE, (me // 4) % 2, (me // 2) % 2, me % 2

    def at(zz, yy, xx, cc):
        return zz * PLANE + yy * 4 + xx * 2 + cc

    zs = [(z + d) % LEVELS for d in (0, 1, 3, 2)]
    x_nbr, y_nbr, core = at(z, y, 1 - x, c), at(z, 1 - y, x, c), at(z, y, x, 1 - c)
    z_nbrs = [at(zz, y, x, c) for zz in zs[1:]]

    barrier = pltpu.get_barrier_semaphore()
    greeted = [x_nbr, y_nbr, core] + z_nbrs
    for other in greeted:
        pl.semaphore_signal(barrier, inc=1, device_id={"seq": other}, device_id_type=MESH)
    own_rows = pl.ds(pl.multiple_of(me * shard, shard), shard)
    moves = [
        (k_ref, kg.at[own_rows, :]), (v_ref, vg.at[own_rows, :]), (q_hbm, q_ref), (pattern_hbm, pattern_ref),
        (counts_hbm, counts_ref), (fine_hbm, fine_ref), (gain_hbm, gain_ref), (win_hbm, win), (wout_hbm, wout),
    ]
    loads = [pltpu.make_async_copy(a, b, load_sem.at[i]) for i, (a, b) in enumerate(moves)]
    for load in loads:
        load.start()
    pl.semaphore_wait(barrier, len(greeted))

    gathered = (kg, vg)
    sent = []

    def rows_of(origin):
        return pl.ds(pl.multiple_of(origin * shard, shard), shard)

    def copy_of(kind, origin, target, own=False):
        place = gathered[kind].at[rows_of(origin), :]
        source = (k_ref, v_ref)[kind] if own else place
        return pltpu.make_async_remote_copy(
            src_ref=source, dst_ref=place,
            send_sem=send_sem.at[len(sent)], recv_sem=recv_sem.at[kind, origin],
            device_id={"seq": target}, device_id_type=MESH,
        )

    def send(kind, origin, target, own=False):
        copy = copy_of(kind, origin, target, own)
        copy.start()
        sent.append(copy)

    def arrive(kind, origin):
        pltpu.make_async_remote_copy(
            src_ref=gathered[kind].at[rows_of(origin), :], dst_ref=gathered[kind].at[rows_of(origin), :],
            send_sem=send_sem.at[0], recv_sem=recv_sem.at[kind, origin],
            device_id={"seq": core}, device_id_type=MESH,
        ).wait_recv()

    def column(level):
        origin = at(zs[level], y, x, c)
        own = level == 0
        for kind in (0, 1):
            if not own:
                arrive(kind, origin)
            for target in (x_nbr, y_nbr, core):
                send(kind, origin, target, own)

    def beside(level):
        by_y, by_x = at(zs[level], 1 - y, x, c), at(zs[level], y, 1 - x, c)
        arrive(0, by_y)
        send(0, by_y, x_nbr)
        send(0, by_y, core)
        arrive(0, by_x)
        send(0, by_x, core)
        arrive(1, by_x)
        send(1, by_x, y_nbr)
        send(1, by_x, core)
        arrive(1, by_y)
        send(1, by_y, core)

    def across(level):
        origin = at(zs[level], 1 - y, 1 - x, c)
        for kind in (0, 1):
            arrive(kind, origin)
            send(kind, origin, core)

    for kind in (0, 1):
        for target in z_nbrs:
            send(kind, me, target, True)
    for turn in range(LEVELS + 2):
        if turn < LEVELS:
            column(turn)
        if 0 <= turn - 1 < LEVELS:
            beside(turn - 1)
        if 0 <= turn - 2 < LEVELS:
            across(turn - 2)
    def arrive_core(kind):
        for zz in zs:
            for yy in (y, 1 - y):
                for xx in (x, 1 - x):
                    arrive(kind, at(zz, yy, xx, 1 - c))

    arrive_core(0)
    for load in loads[:6]:
        load.wait()
    own = pl.multiple_of(z * KBLK, KBLK)
    others = [pl.multiple_of(zz * KBLK, KBLK) for zz in zs[1:]]
    second = jnp.broadcast_to(pattern_ref[:, 1:2], (1, 2 * HEAD))
    picks = [jnp.where(second == zz, 1.0, 0.0).astype(jnp.bfloat16) for zz in zs[1:]]
    used = jnp.broadcast_to(counts_ref[...], (1, KBLK))
    bias = jnp.concatenate([jnp.zeros((1, KBLK), jnp.float32), jnp.where(used > 1, 0.0, -1e30)], axis=1)
    for pair in range(q_ref.shape[1] // (2 * HEAD)):
        weigh_pair(q_ref, kg, weights, own, others, picks, bias, pair)
    arrive_core(1)
    for pair in range(q_ref.shape[1] // (2 * HEAD)):
        attend_pair(weights, vg, fine_ref, mid, own, others, picks, pair)
    loads[6].wait()
    feed_forward(mid, gain_ref, win, wout, hid, out_ref, loads[7].wait, loads[8].wait)
    for copy in sent:
        copy.wait_send()


def fast_shards(fine, queries, keys, values, pattern, counts, norm_gain, w_in, w_out):
    rows, width = fine.shape
    hidden = w_in.shape[1]
    gathered = (keys.shape[0] * lax.axis_size("seq"), width)
    vmem = pl.BlockSpec(memory_space=pltpu.VMEM)
    hbm = pl.BlockSpec(memory_space=pl.ANY)
    sends = 6 + LEVELS * (6 + 6 + 2)
    return pl.pallas_call(
        kernel,
        out_shape=jax.ShapeDtypeStruct((rows, width), jnp.bfloat16),
        in_specs=[hbm] * 9,
        out_specs=vmem,
        scratch_shapes=[
            pltpu.VMEM(pattern.shape, jnp.int32),
            pltpu.VMEM((1, 1), jnp.int32),
            pltpu.VMEM(queries.shape, jnp.bfloat16),
            pltpu.VMEM(fine.shape, jnp.bfloat16),
            pltpu.VMEM((1, width), jnp.float32),
            pltpu.VMEM(gathered, jnp.bfloat16),
            pltpu.VMEM(gathered, jnp.bfloat16),
            pltpu.VMEM(w_in.shape, jnp.bfloat16),
            pltpu.VMEM(w_out.shape, jnp.bfloat16),
            pltpu.VMEM((rows, width), jnp.float32),
            pltpu.VMEM((rows, hidden), jnp.bfloat16),
            pltpu.VMEM((width // (2 * HEAD), 2 * rows, 2 * KBLK), jnp.bfloat16),
            pltpu.SemaphoreType.DMA((9,)),
            pltpu.SemaphoreType.DMA((sends,)),
            pltpu.SemaphoreType.DMA((2, gathered[0] // keys.shape[0])),
        ],
        compiler_params=pltpu.CompilerParams(
            collective_id=0, has_side_effects=True, vmem_limit_bytes=58 * 2**20
        ),
        cost_estimate=pl.CostEstimate(
            flops=4 * rows * width * hidden, bytes_accessed=4 * width * hidden, transcendentals=rows * hidden
        ),
    )(pattern, counts.reshape(1, 1), queries, keys, values, fine, norm_gain.reshape(1, -1), w_in, w_out)


def shards(fine, queries, keys, values, pattern, counts, norm_gain, w_in, w_out):
    local_rows, half_width = queries.shape
    head_count = half_width // HEAD
    scale_factor = 1.0 / math.sqrt(HEAD)
    query_heads = queries.reshape(local_rows, head_count, HEAD)
    slot_count = pattern.shape[1]
    block_total = keys.shape[0] * lax.axis_size("seq") // KBLK
    slot_live = jnp.arange(slot_count, dtype=jnp.int32)[None, :] < counts[:, None]
    block_ids = jnp.arange(block_total, dtype=jnp.int32)
    chosen = jnp.any(
        (pattern[:, :, None] == block_ids[None, None, :]) & slot_live[:, :, None], axis=1
    )

    def absorb(running, key_rows, value_rows, first_row):
        width = key_rows.shape[0]
        row_block = (first_row + jnp.arange(width, dtype=jnp.int32)) // KBLK
        allowed = jnp.any(
            chosen[:, None, :] & (row_block[:, None] == block_ids[None, :])[None, :, :], axis=2
        )
        allowed = jnp.repeat(allowed, QBLK, axis=0)[None, :, :]
        maxima, totals, weighted = running
        scores = (
            jnp.einsum(
                "qhd,khd->hqk",
                query_heads,
                key_rows.reshape(width, head_count, HEAD),
                preferred_element_type=jnp.float32,
            )
            * scale_factor
        )
        piece_max = jnp.max(jnp.where(allowed, scores, -1e30), axis=2)
        new_max = jnp.maximum(maxima, piece_max)
        probs = jnp.where(
            allowed, jnp.exp(jnp.where(allowed, scores - new_max[:, :, None], -1e30)), 0.0
        )
        factor = jnp.exp(maxima - new_max)
        totals = totals * factor + jnp.sum(probs, axis=2)
        update = jnp.einsum(
            "hqk,khd->qhd",
            probs.astype(jnp.bfloat16),
            value_rows.reshape(width, head_count, HEAD),
            preferred_element_type=jnp.float32,
        )
        weighted = weighted * jnp.transpose(factor)[:, :, None] + update
        return (new_max, totals, weighted)

    initial = (
        jnp.full((head_count, local_rows), -1e30, jnp.float32),
        jnp.zeros((head_count, local_rows), jnp.float32),
        jnp.zeros((local_rows, head_count, HEAD), jnp.float32),
    )
    key_piece = lax.all_gather(keys, "seq", axis=0, tiled=True)
    value_piece = lax.all_gather(values, "seq", axis=0, tiled=True)
    width = key_piece.shape[0]
    span = 512

    def inner(turn, state):
        offset = turn * span
        return absorb(
            state,
            lax.dynamic_slice_in_dim(key_piece, offset, span, 0),
            lax.dynamic_slice_in_dim(value_piece, offset, span, 0),
            offset,
        )

    maxima, totals, weighted = lax.fori_loop(0, width // span, inner, initial)
    attn = (
        (weighted / jnp.transpose(totals)[:, :, None])
        .astype(jnp.bfloat16)
        .reshape(local_rows, half_width)
    )
    moved_fine, moved_attn = (
        lax.all_to_all(fine, "fsdp", split_axis=0, concat_axis=1, tiled=True),
        lax.all_to_all(attn, "fsdp", split_axis=0, concat_axis=1, tiled=True),
    )
    middle = moved_fine.astype(jnp.float32) + moved_attn.astype(jnp.float32)
    mean_square = jnp.mean(middle * middle, axis=1, keepdims=True)
    normed = (middle * lax.rsqrt(mean_square + 1e-06) * norm_gain).astype(jnp.bfloat16)
    before = jnp.dot(
        normed, lax.all_gather(w_in, "fsdp", axis=0, tiled=True), preferred_element_type=jnp.float32
    )
    hidden = jax.nn.gelu(before, approximate=True).astype(jnp.bfloat16)
    output_sum = jnp.dot(
        hidden,
        lax.all_gather(w_out, "fsdp", axis=0, tiled=True),
        preferred_element_type=jnp.float32,
    )
    return (middle + output_sum).astype(jnp.bfloat16)

def is_small(mesh):
    return mesh.shape["groups"] == 1 and mesh.shape["fsdp"] == 1 and mesh.shape["seq"] == PLANE * LEVELS


def solution(mesh):
    return jax.shard_map(
        fast_shards if is_small(mesh) else shards,
        mesh=mesh,
        in_specs=(
            P(("groups", "seq"), "fsdp"),
            P(("groups", "seq"), "fsdp"),
            P(("groups", "seq"), "fsdp"),
            P(("groups", "seq"), "fsdp"),
            P(("groups", "seq"), None),
            P(("groups", "seq")),
            P(),
            P("fsdp", None),
            P("fsdp", None),
        ),
        out_specs=P(("groups", "seq", "fsdp"), None),
        check_vma=False,
    )
```

```python
import functools
import math

import jax
import jax.numpy as jnp
from jax import lax
from jax.experimental import pallas as pl
from jax.experimental.pallas import tpu as pltpu
from jax.sharding import PartitionSpec as P

HEAD = 64
QBLK = 128
KBLK = 128
MESH = pl.DeviceIdType.MESH
PLANE = 8
LEVELS = 4


def choose(ref, others, picks, columns):
    block = None
    for start, pick in zip(others, picks):
        part = ref[pl.ds(start, KBLK), columns] * pick
        block = part if block is None else block + part
    return block


def weigh_pair(q_ref, k_ref, weight_ref, own, others, picks, bias, pair):
    columns = pl.ds(pair * 2 * HEAD, 2 * HEAD)
    q = q_ref[:, columns] * jnp.bfloat16(1.0 / math.sqrt(HEAD))
    lane = lax.broadcasted_iota(jnp.int32, q.shape, 1)
    zero = jnp.zeros_like(q)
    both = jnp.concatenate([jnp.where(lane < HEAD, q, zero), jnp.where(lane < HEAD, zero, q)], axis=0)
    k = jnp.concatenate([k_ref[pl.ds(own, KBLK), columns], choose(k_ref, others, picks, columns)], axis=0)
    s = lax.dot_general(both, k, (((1,), (1,)), ((), ())), preferred_element_type=jnp.float32) + bias
    top = jnp.max(s, axis=1, keepdims=True)
    weight_ref[pair] = jnp.exp(s - top).astype(jnp.bfloat16)


def attend_pair(weight_ref, v_ref, fine_ref, mid_ref, own, others, picks, pair):
    columns = pl.ds(pair * 2 * HEAD, 2 * HEAD)
    weights = weight_ref[pair]
    v = jnp.concatenate([v_ref[pl.ds(own, KBLK), columns], choose(v_ref, others, picks, columns)], axis=0)
    v = jnp.concatenate([v, jnp.ones_like(v)], axis=1)
    summed = jnp.dot(weights, v, preferred_element_type=jnp.float32)
    out = summed[:, : 2 * HEAD] / summed[:, 2 * HEAD :]
    rows = fine_ref.shape[0]
    lane = lax.broadcasted_iota(jnp.int32, (rows, 2 * HEAD), 1)
    out = jnp.where(lane < HEAD, out[:rows], out[rows:]).astype(jnp.bfloat16)
    mid_ref[:, columns] = fine_ref[:, columns].astype(jnp.float32) + out.astype(jnp.float32)


def feed_forward(mid_ref, gain_ref, win, wout, hid_ref, out_ref, wait_in, wait_out):
    mid = mid_ref[...]
    mean_square = jnp.mean(mid * mid, axis=1, keepdims=True)
    normed = (mid * lax.rsqrt(mean_square + 1e-06) * gain_ref[...]).astype(jnp.bfloat16)
    wait_in()
    step = 256
    for c in range(hid_ref.shape[1] // step):
        cols = pl.ds(c * step, step)
        before = jnp.dot(normed, win[:, cols], preferred_element_type=jnp.float32)
        hid_ref[:, cols] = jax.nn.gelu(before, approximate=True).astype(jnp.bfloat16)
    wait_out()
    for c in range(out_ref.shape[1] // step):
        cols = pl.ds(c * step, step)
        y = jnp.dot(hid_ref[...], wout[:, cols], preferred_element_type=jnp.float32)
        out_ref[:, cols] = (mid_ref[:, cols] + y).astype(jnp.bfloat16)


def kernel(
    pattern_hbm, counts_hbm, q_hbm, k_ref, v_ref, fine_hbm, gain_hbm, win_hbm, wout_hbm,
    out_ref,
    pattern_ref, counts_ref, q_ref, fine_ref, gain_ref, kg, vg, win, wout, mid, hid, weights, load_sem, send_sem, recv_sem,
):
    me = lax.axis_index("seq")
    shard = k_ref.shape[0]
    z, y, x, c = me // PLANE, (me // 4) % 2, (me // 2) % 2, me % 2

    def at(zz, yy, xx, cc):
        return zz * PLANE + yy * 4 + xx * 2 + cc

    zs = [(z + d) % LEVELS for d in (0, 1, 3, 2)]
    x_nbr, y_nbr, core = at(z, y, 1 - x, c), at(z, 1 - y, x, c), at(z, y, x, 1 - c)
    z_nbrs = [at(zz, y, x, c) for zz in zs[1:]]

    barrier = pltpu.get_barrier_semaphore()
    greeted = [x_nbr, y_nbr, core] + z_nbrs
    for other in greeted:
        pl.semaphore_signal(barrier, inc=1, device_id={"seq": other}, device_id_type=MESH)
    own_rows = pl.ds(pl.multiple_of(me * shard, shard), shard)
    moves = [
        (k_ref, kg.at[own_rows, :]), (v_ref, vg.at[own_rows, :]), (q_hbm, q_ref), (pattern_hbm, pattern_ref),
        (counts_hbm, counts_ref), (fine_hbm, fine_ref), (gain_hbm, gain_ref), (win_hbm, win), (wout_hbm, wout),
    ]
    loads = [pltpu.make_async_copy(a, b, load_sem.at[i]) for i, (a, b) in enumerate(moves)]
    for load in loads:
        load.start()
    pl.semaphore_wait(barrier, len(greeted))

    gathered = (kg, vg)
    sent = []

    def rows_of(origin):
        return pl.ds(pl.multiple_of(origin * shard, shard), shard)

    def copy_of(kind, origin, target, own=False):
        place = gathered[kind].at[rows_of(origin), :]
        source = (k_ref, v_ref)[kind] if own else place
        return pltpu.make_async_remote_copy(
            src_ref=source, dst_ref=place,
            send_sem=send_sem.at[len(sent)], recv_sem=recv_sem.at[kind, origin],
            device_id={"seq": target}, device_id_type=MESH,
        )

    def send(kind, origin, target, own=False):
        copy = copy_of(kind, origin, target, own)
        copy.start()
        sent.append(copy)

    def arrive(kind, origin):
        pltpu.make_async_remote_copy(
            src_ref=gathered[kind].at[rows_of(origin), :], dst_ref=gathered[kind].at[rows_of(origin), :],
            send_sem=send_sem.at[0], recv_sem=recv_sem.at[kind, origin],
            device_id={"seq": core}, device_id_type=MESH,
        ).wait_recv()

    def column(level):
        origin = at(zs[level], y, x, c)
        own = level == 0
        for kind in (0, 1):
            if not own:
                arrive(kind, origin)
            for target in (x_nbr, y_nbr, core):
                send(kind, origin, target, own)

    def beside(level):
        by_y, by_x = at(zs[level], 1 - y, x, c), at(zs[level], y, 1 - x, c)
        arrive(0, by_y)
        send(0, by_y, x_nbr)
        send(0, by_y, core)
        arrive(0, by_x)
        send(0, by_x, core)
        arrive(1, by_x)
        send(1, by_x, y_nbr)
        send(1, by_x, core)
        arrive(1, by_y)
        send(1, by_y, core)

    def across(level):
        origin = at(zs[level], 1 - y, 1 - x, c)
        for kind in (0, 1):
            arrive(kind, origin)
            send(kind, origin, core)

    for target in z_nbrs:
        for kind in (0, 1):
            send(kind, me, target, True)
    for turn in range(LEVELS + 4):
        if turn < LEVELS:
            column(turn)
        if 0 <= turn - 2 < LEVELS:
            beside(turn - 2)
        if 0 <= turn - 4 < LEVELS:
            across(turn - 4)

    def arrive_core(kind):
        for zz in zs:
            for yy in (y, 1 - y):
                for xx in (x, 1 - x):
                    arrive(kind, at(zz, yy, xx, 1 - c))

    arrive_core(0)
    for load in loads[:6]:
        load.wait()
    own = pl.multiple_of(z * KBLK, KBLK)
    others = [pl.multiple_of(zz * KBLK, KBLK) for zz in zs[1:]]
    second = jnp.broadcast_to(pattern_ref[:, 1:2], (1, 2 * HEAD))
    picks = [jnp.where(second == zz, 1.0, 0.0).astype(jnp.bfloat16) for zz in zs[1:]]
    used = jnp.full((1, KBLK), counts_ref[0], jnp.int32)
    bias = jnp.concatenate([jnp.zeros((1, KBLK), jnp.float32), jnp.where(used > 1, 0.0, -1e30)], axis=1)
    for pair in range(q_ref.shape[1] // (2 * HEAD)):
        weigh_pair(q_ref, kg, weights, own, others, picks, bias, pair)
    arrive_core(1)
    for pair in range(q_ref.shape[1] // (2 * HEAD)):
        attend_pair(weights, vg, fine_ref, mid, own, others, picks, pair)
    loads[6].wait()
    feed_forward(mid, gain_ref, win, wout, hid, out_ref, loads[7].wait, loads[8].wait)
    for copy in sent:
        copy.wait_send()


def fast_shards(fine, queries, keys, values, pattern, counts, norm_gain, w_in, w_out):
    rows, width = fine.shape
    hidden = w_in.shape[1]
    gathered = (keys.shape[0] * lax.axis_size("seq"), width)
    vmem = pl.BlockSpec(memory_space=pltpu.VMEM)
    hbm = pl.BlockSpec(memory_space=pl.ANY)
    sends = 6 + LEVELS * (6 + 6 + 2)
    return pl.pallas_call(
        kernel,
        out_shape=jax.ShapeDtypeStruct((rows, width), jnp.bfloat16),
        in_specs=[hbm] * 9,
        out_specs=vmem,
        scratch_shapes=[
            pltpu.VMEM(pattern.shape, jnp.int32),
            pltpu.SMEM(counts.shape, jnp.int32),
            pltpu.VMEM(queries.shape, jnp.bfloat16),
            pltpu.VMEM(fine.shape, jnp.bfloat16),
            pltpu.VMEM((1, width), jnp.float32),
            pltpu.VMEM(gathered, jnp.bfloat16),
            pltpu.VMEM(gathered, jnp.bfloat16),
            pltpu.VMEM(w_in.shape, jnp.bfloat16),
            pltpu.VMEM(w_out.shape, jnp.bfloat16),
            pltpu.VMEM((rows, width), jnp.float32),
            pltpu.VMEM((rows, hidden), jnp.bfloat16),
            pltpu.VMEM((width // (2 * HEAD), 2 * rows, 2 * KBLK), jnp.bfloat16),
            pltpu.SemaphoreType.DMA((9,)),
            pltpu.SemaphoreType.DMA((sends,)),
            pltpu.SemaphoreType.DMA((2, gathered[0] // keys.shape[0])),
        ],
        compiler_params=pltpu.CompilerParams(
            collective_id=0, has_side_effects=True, vmem_limit_bytes=58 * 2**20
        ),
        cost_estimate=pl.CostEstimate(
            flops=4 * rows * width * hidden, bytes_accessed=4 * width * hidden, transcendentals=rows * hidden
        ),
    )(pattern, counts, queries, keys, values, fine, norm_gain.reshape(1, -1), w_in, w_out)


def shards(fine, queries, keys, values, pattern, counts, norm_gain, w_in, w_out):
    local_rows, half_width = queries.shape
    head_count = half_width // HEAD
    scale_factor = 1.0 / math.sqrt(HEAD)
    query_heads = queries.reshape(local_rows, head_count, HEAD)
    slot_count = pattern.shape[1]
    block_total = keys.shape[0] * lax.axis_size("seq") // KBLK
    slot_live = jnp.arange(slot_count, dtype=jnp.int32)[None, :] < counts[:, None]
    block_ids = jnp.arange(block_total, dtype=jnp.int32)
    chosen = jnp.any(
        (pattern[:, :, None] == block_ids[None, None, :]) & slot_live[:, :, None], axis=1
    )

    def absorb(running, key_rows, value_rows, first_row):
        width = key_rows.shape[0]
        row_block = (first_row + jnp.arange(width, dtype=jnp.int32)) // KBLK
        allowed = jnp.any(
            chosen[:, None, :] & (row_block[:, None] == block_ids[None, :])[None, :, :], axis=2
        )
        allowed = jnp.repeat(allowed, QBLK, axis=0)[None, :, :]
        maxima, totals, weighted = running
        scores = (
            jnp.einsum(
                "qhd,khd->hqk",
                query_heads,
                key_rows.reshape(width, head_count, HEAD),
                preferred_element_type=jnp.float32,
            )
            * scale_factor
        )
        piece_max = jnp.max(jnp.where(allowed, scores, -1e30), axis=2)
        new_max = jnp.maximum(maxima, piece_max)
        probs = jnp.where(
            allowed, jnp.exp(jnp.where(allowed, scores - new_max[:, :, None], -1e30)), 0.0
        )
        factor = jnp.exp(maxima - new_max)
        totals = totals * factor + jnp.sum(probs, axis=2)
        update = jnp.einsum(
            "hqk,khd->qhd",
            probs.astype(jnp.bfloat16),
            value_rows.reshape(width, head_count, HEAD),
            preferred_element_type=jnp.float32,
        )
        weighted = weighted * jnp.transpose(factor)[:, :, None] + update
        return (new_max, totals, weighted)

    initial = (
        jnp.full((head_count, local_rows), -1e30, jnp.float32),
        jnp.zeros((head_count, local_rows), jnp.float32),
        jnp.zeros((local_rows, head_count, HEAD), jnp.float32),
    )
    key_piece = lax.all_gather(keys, "seq", axis=0, tiled=True)
    value_piece = lax.all_gather(values, "seq", axis=0, tiled=True)
    width = key_piece.shape[0]
    span = 512

    def inner(turn, state):
        offset = turn * span
        return absorb(
            state,
            lax.dynamic_slice_in_dim(key_piece, offset, span, 0),
            lax.dynamic_slice_in_dim(value_piece, offset, span, 0),
            offset,
        )

    maxima, totals, weighted = lax.fori_loop(0, width // span, inner, initial)
    attn = (
        (weighted / jnp.transpose(totals)[:, :, None])
        .astype(jnp.bfloat16)
        .reshape(local_rows, half_width)
    )
    moved_fine, moved_attn = (
        lax.all_to_all(fine, "fsdp", split_axis=0, concat_axis=1, tiled=True),
        lax.all_to_all(attn, "fsdp", split_axis=0, concat_axis=1, tiled=True),
    )
    middle = moved_fine.astype(jnp.float32) + moved_attn.astype(jnp.float32)
    mean_square = jnp.mean(middle * middle, axis=1, keepdims=True)
    normed = (middle * lax.rsqrt(mean_square + 1e-06) * norm_gain).astype(jnp.bfloat16)
    before = jnp.dot(
        normed, lax.all_gather(w_in, "fsdp", axis=0, tiled=True), preferred_element_type=jnp.float32
    )
    hidden = jax.nn.gelu(before, approximate=True).astype(jnp.bfloat16)
    output_sum = jnp.dot(
        hidden,
        lax.all_gather(w_out, "fsdp", axis=0, tiled=True),
        preferred_element_type=jnp.float32,
    )
    return (middle + output_sum).astype(jnp.bfloat16)

def is_small(mesh):
    return mesh.shape["groups"] == 1 and mesh.shape["fsdp"] == 1 and mesh.shape["seq"] == PLANE * LEVELS


def solution(mesh):
    return jax.shard_map(
        fast_shards if is_small(mesh) else shards,
        mesh=mesh,
        in_specs=(
            P(("groups", "seq"), "fsdp"),
            P(("groups", "seq"), "fsdp"),
            P(("groups", "seq"), "fsdp"),
            P(("groups", "seq"), "fsdp"),
            P(("groups", "seq"), None),
            P(("groups", "seq")),
            P(),
            P("fsdp", None),
            P("fsdp", None),
        ),
        out_specs=P(("groups", "seq", "fsdp"), None),
        check_vma=False,
    )
```
